768 devices in a mesh: tok: 192 (over z, y, core), wid: 4 (over x).
Axes of the slice: x: 4, y: 8, z: 12, core: 2. Of those that a mesh axis runs over, the one named last changes fastest.
Arguments:
- activations: bfloat16 [49152, 8192], P('tok', 'wid'), may hold values from -180 to 180
- sketch: bfloat16 [8192, 256], P('wid'), may hold values from -6 to 6
Outputs:
- new_basis: bfloat16 [8192, 256], P('wid')
The draws below stay inside these ranges and needn't reach their ends.
All inputs are finite; a program needn't handle non-finite values.
Results may differ from the reference program's by a relative error of at most 0.0034.
Values may be sent and summed in bfloat16 or wider, within the bound.
No kernel may reach another device: no remote copies, remote signals or barrier semaphores. Data moves between devices by JAX's collectives and lax.ppermute only.
A program may use at most 32 MiB of HBM per device.

```python
import math
import jax
import jax.numpy as jnp
from jax import lax

D = 8192
K = 256
TOKENS = 49152


def draw_activations(key, part):
    first, second, third = jax.random.split(key, 3)
    base = jnp.clip(jax.random.normal(first, (TOKENS, D), jnp.float32), -6.0, 6.0)
    row_scale = jnp.exp(jax.random.uniform(second, (TOKENS,), jnp.float32, 0.0, 2.3026))
    col_scale = jnp.exp(jax.random.uniform(third, (D,), jnp.float32, 0.0, 1.0986))
    return (base * row_scale[:, None] * col_scale[None, :]).astype(jnp.bfloat16)


def block_scale(stream_key, extent, shards, smallest, high):
    gain, own = 1.0, jax.random.fold_in(stream_key, 6)
    for position, blocks in shards:
        steps = jnp.exp(jax.random.uniform(jax.random.fold_in(own, position), (blocks,), jnp.float32, smallest / len(shards), high / len(shards)))
        gain = gain * jnp.repeat(steps, extent[position] // blocks).reshape([-1 if axis == position else 1 for axis in range(len(extent))])
    return gain


def bell_draw(stream_key, dims, deviation, most, cuts=(), kind=jnp.bfloat16):
    drawn = jax.random.normal(stream_key, dims, jnp.float32) * deviation
    if len(cuts) > 0:
        drawn = block_scale(stream_key, dims, cuts, -0.22, 0.18) * drawn
    return jnp.clip(drawn, min=-most, max=most).astype(kind)


def setup_inputs(seed: int = 0) -> dict:
    streams_of = jax.random.split(jax.random.key(seed), 3)
    activations = draw_activations(jax.random.fold_in(streams_of[2], 71), 0)
    sketch = bell_draw(streams_of[1], (D, K), 1.0, 6.0, ((0, 4),))
    return dict(activations=activations, sketch=sketch)


def reference(activations, sketch):
    partial_sum = jnp.dot(activations.astype(jnp.float32), sketch.astype(jnp.float32), preferred_element_type=jnp.float32)
    projected = (partial_sum * (1.0 / math.sqrt(D))).astype(jnp.bfloat16)
    moment = lax.dot_general(activations.astype(jnp.float32), projected.astype(jnp.float32), (((0,), (0,)), ((), ())), preferred_element_type=jnp.float32) / TOKENS
    gram = jnp.dot(moment.T, moment, precision=lax.Precision.HIGHEST)
    lower = jnp.linalg.cholesky(gram)
    solved = lax.linalg.triangular_solve(lower, moment, left_side=False, lower=True, transpose_a=True)
    return (solved * math.sqrt(D)).astype(jnp.bfloat16)
```

```python
import math

import jax
import jax.numpy as jnp
from jax import lax
from jax.experimental import pallas as pl
from jax.experimental.pallas import tpu as pltpu
from jax.sharding import Mesh, PartitionSpec as P

D = 8192
K = 256
TOKENS = 49152
BLOCK = 8
TOK = ("zh", "zl", "y", "core")


def inverse_factor_kernel(gram_ref, out_ref, work):
    work[...] = gram_ref[...]
    lane = lax.broadcasted_iota(jnp.int32, (BLOCK, K), 1)
    row_of = lax.broadcasted_iota(jnp.int32, (BLOCK, K), 0)
    for j in range(0, K, BLOCK):
        inside = (lane >= j) & (lane < j + BLOCK)
        rows = work[j : j + BLOCK, :]
        columns = [jnp.broadcast_to(rows[:, j + c : j + c + 1], (BLOCK, 128)) for c in range(BLOCK)]
        left = {
            (r, c): jnp.broadcast_to(columns[c][r : r + 1, :], (BLOCK, 128))
            for c in range(BLOCK)
            for r in range(c, BLOCK)
        }
        scale, low = [], {}
        for t in range(BLOCK):
            inv = lax.rsqrt(left[t, t])
            scale.append(jnp.concatenate([inv, inv], axis=1))
            narrow = {r: left[r, t] * inv for r in range(t + 1, BLOCK)}
            for c in range(t + 1, BLOCK):
                for r in range(c, BLOCK):
                    left[r, c] = left[r, c] - narrow[r] * narrow[c]
            for r, value in narrow.items():
                low[r, t] = jnp.concatenate([value, value], axis=1)
        solved = []
        for t in range(BLOCK):
            row = jnp.broadcast_to(rows[t : t + 1, :], (BLOCK, K))
            row = jnp.where(inside, jnp.where(lane == j + t, 1.0, 0.0), row)
            for s in range(t):
                row = row - low[t, s] * solved[s]
            solved.append(row * scale[t])
        if j + BLOCK < K:
            update = [None] * BLOCK
            for t in reversed(range(BLOCK)):
                row = solved[t]
                for s in range(t + 1, BLOCK):
                    row = row - low[s, t] * update[s]
                update[t] = row * scale[t]
            for i in range(j + BLOCK, K, BLOCK):
                below = work[i : i + BLOCK, :]
                new = jnp.where(inside, 0.0, below)
                for t in range(BLOCK):
                    new = new - jnp.broadcast_to(below[:, j + t : j + t + 1], (BLOCK, K)) * update[t]
                work[i : i + BLOCK, :] = new
        result = solved[0]
        for t in range(1, BLOCK):
            result = jnp.where(row_of == t, solved[t], result)
        out_ref[j : j + BLOCK, :] = jnp.where(lane < j + BLOCK, result, 0.0)


def inverse_factor(gram):
    return pl.pallas_call(
        inverse_factor_kernel,
        out_shape=jax.ShapeDtypeStruct((K, K), jnp.float32),
        in_specs=[pl.BlockSpec(memory_space=pltpu.VMEM)],
        out_specs=pl.BlockSpec(memory_space=pltpu.VMEM),
        scratch_shapes=[pltpu.VMEM((K, K), jnp.float32)],
        cost_estimate=pl.CostEstimate(flops=40_000_000, bytes_accessed=524_288, transcendentals=K),
    )(gram)


def swap(pieces, axis):
    return lax.all_to_all(pieces, axis, 0, 0, tiled=True)


def share(block, axis):
    return swap(jnp.broadcast_to(block[None], (lax.axis_size(axis),) + block.shape), axis)


def on_device(activations, sketch):
    tok_rows, panel = activations.shape
    half = panel // 2
    core = lax.axis_index("core")
    kept = lax.dynamic_slice_in_dim(activations, core * half, half, axis=1)
    given = lax.dynamic_slice_in_dim(activations, (1 - core) * half, half, axis=1)
    other = lax.ppermute(given, "core", [(0, 1), (1, 0)])

    with jax.named_scope("projected"):
        partial_sum = jnp.dot(activations, sketch, preferred_element_type=jnp.float32)
        summed = jnp.sum(swap(partial_sum.reshape(4, tok_rows // 4, K), "x"), axis=0)
        rows = (summed * (1.0 / math.sqrt(D))).astype(jnp.bfloat16)
        projected = share(rows, ("core", "x")).reshape(2, tok_rows, K)
        own = lax.dynamic_index_in_dim(projected, core, axis=0, keepdims=False)
        others = lax.dynamic_index_in_dim(projected, 1 - core, axis=0, keepdims=False)

    with jax.named_scope("moment"):
        over_tokens = (((0,), (0,)), ((), ()))
        chip_sum = lax.dot_general(
            kept, own, over_tokens, preferred_element_type=jnp.float32
        ) + lax.dot_general(other, others, over_tokens, preferred_element_type=jnp.float32)
        pieces = chip_sum.astype(jnp.bfloat16).reshape(8, half // 8, K)
        piece = jnp.sum(swap(pieces, "y").astype(jnp.float32), axis=0)
        part = jnp.sum(swap(piece.reshape(4, half // 32, K), "zl"), axis=0)
        part = jnp.sum(share(part, "zh"), axis=0)
        moment = share(part, "zl").reshape(half // 8, K) / TOKENS
        whole = lax.all_gather(moment, ("core", "y"), axis=0, tiled=True)

    with jax.named_scope("gram"):
        local_gram = lax.dot_general(
            moment, moment, over_tokens, precision=lax.Precision.HIGHEST
        )
        strip = jnp.sum(swap(local_gram.reshape(8, K // 8, K), ("core", "x")), axis=0)
        strip = jnp.sum(share(strip, "y"), axis=0)
        gram = share(strip, ("core", "x")).reshape(K, K)

    with jax.named_scope("new_basis"):
        inverse = inverse_factor(gram)
        solved = lax.dot_general(
            whole, inverse, (((1,), (1,)), ((), ())), precision=lax.Precision.HIGHEST
        )
        return (solved * math.sqrt(D)).astype(jnp.bfloat16)


def solution(mesh):
    fine = Mesh(mesh.devices.reshape(3, 4, 8, 2, 4), TOK + ("x",))
    return jax.shard_map(
        on_device,
        mesh=fine,
        in_specs=(P(TOK, "x"), P("x", None)),
        out_specs=P("x", None),
        check_vma=False,
    )
```

```python
import math

import jax
import jax.numpy as jnp
from jax import lax
from jax.experimental import pallas as pl
from jax.experimental.pallas import tpu as pltpu
from jax.sharding import Mesh, PartitionSpec as P

D = 8192
K = 256
TOKENS = 49152
BLOCK = 8
TOK = ("zh", "zl", "y", "core")


def inverse_factor_kernel(gram_ref, out_ref, work):
    work[...] = gram_ref[...]
    lane = lax.broadcasted_iota(jnp.int32, (BLOCK, K), 1)
    row_of = lax.broadcasted_iota(jnp.int32, (BLOCK, K), 0)

    def wide(value):
        return jnp.concatenate([value, value], axis=1)

    def column(block, k):
        return jnp.broadcast_to(block[:, k : k + 1], (BLOCK, 128))

    for j in range(0, K, BLOCK):
        inside = (lane >= j) & (lane < j + BLOCK)
        rows = work[j : j + BLOCK, :]
        columns = [column(rows, j + c) for c in range(BLOCK)]
        left = {
            (r, c): jnp.broadcast_to(columns[c][r : r + 1, :], (BLOCK, 128))
            for c in range(BLOCK)
            for r in range(c, BLOCK)
        }
        near = j + BLOCK if j + BLOCK < K else None
        if near is not None:
            below = work[near : near + BLOCK, :]
            below_columns = [column(below, j + c) for c in range(BLOCK)]
            new = jnp.where(inside, 0.0, below)
        scale, low, solved = [], {}, []
        for t in range(BLOCK):
            inv = lax.rsqrt(left[t, t])
            narrow = {r: left[r, t] * inv for r in range(t + 1, BLOCK)}
            for c in range(t + 1, BLOCK):
                for r in range(c, BLOCK):
                    left[r, c] = left[r, c] - narrow[r] * narrow[c]
            for r, value in narrow.items():
                low[r, t] = wide(value)
            scale.append(wide(inv))
            row = jnp.broadcast_to(rows[t : t + 1, :], (BLOCK, K))
            row = jnp.where(inside, jnp.where(lane == j + t, 1.0, 0.0), row)
            for s in range(t):
                row = row - low[t, s] * solved[s]
            solved.append(row * scale[t])
            if near is not None:
                factor = below_columns[t] * inv
                for c in range(t + 1, BLOCK):
                    below_columns[c] = below_columns[c] - factor * narrow[c]
                new = new - wide(factor) * solved[t]
        if near is not None:
            work[near : near + BLOCK, :] = new
        if j + 2 * BLOCK < K:
            update = [None] * BLOCK
            for t in reversed(range(BLOCK)):
                row = solved[t]
                for s in range(t + 1, BLOCK):
                    row = row - low[s, t] * update[s]
                update[t] = row * scale[t]
            for i in range(j + 2 * BLOCK, K, BLOCK):
                below = work[i : i + BLOCK, :]
                new = jnp.where(inside, 0.0, below)
                for t in range(BLOCK):
                    new = new - jnp.broadcast_to(below[:, j + t : j + t + 1], (BLOCK, K)) * update[t]
                work[i : i + BLOCK, :] = new
        result = solved[0]
        for t in range(1, BLOCK):
            result = jnp.where(row_of == t, solved[t], result)
        out_ref[j : j + BLOCK, :] = jnp.where(lane < j + BLOCK, result, 0.0)


def inverse_factor(gram):
    return pl.pallas_call(
        inverse_factor_kernel,
        out_shape=jax.ShapeDtypeStruct((K, K), jnp.float32),
        in_specs=[pl.BlockSpec(memory_space=pltpu.VMEM)],
        out_specs=pl.BlockSpec(memory_space=pltpu.VMEM),
        scratch_shapes=[pltpu.VMEM((K, K), jnp.float32)],
        cost_estimate=pl.CostEstimate(flops=40_000_000, bytes_accessed=524_288, transcendentals=K),
    )(gram)


def swap(pieces, axis):
    return lax.all_to_all(pieces, axis, 0, 0, tiled=True)


def share(block, axis):
    return swap(jnp.broadcast_to(block[None], (lax.axis_size(axis),) + block.shape), axis)


def on_device(activations, sketch):
    tok_rows, panel = activations.shape
    half = panel // 2
    core = lax.axis_index("core")
    kept = lax.dynamic_slice_in_dim(activations, core * half, half, axis=1)
    given = lax.dynamic_slice_in_dim(activations, (1 - core) * half, half, axis=1)
    other = lax.ppermute(given, "core", [(0, 1), (1, 0)])

    with jax.named_scope("projected"):
        partial_sum = jnp.dot(activations, sketch, preferred_element_type=jnp.float32)
        summed = jnp.sum(swap(partial_sum.reshape(4, tok_rows // 4, K), "x"), axis=0)
        rows = (summed * (1.0 / math.sqrt(D))).astype(jnp.bfloat16)
        projected = share(rows, ("core", "x")).reshape(2, tok_rows, K)
        own = lax.dynamic_index_in_dim(projected, core, axis=0, keepdims=False)
        others = lax.dynamic_index_in_dim(projected, 1 - core, axis=0, keepdims=False)

    with jax.named_scope("moment"):
        over_tokens = (((0,), (0,)), ((), ()))
        chip_sum = lax.dot_general(
            kept, own, over_tokens, preferred_element_type=jnp.float32
        ) + lax.dot_general(other, others, over_tokens, preferred_element_type=jnp.float32)
        pieces = chip_sum.astype(jnp.bfloat16).reshape(32, half // 32, K)
        part = jnp.sum(swap(pieces, ("y", "zl")).astype(jnp.float32), axis=0)
        part = jnp.sum(share(part, "zh"), axis=0)
        moment = part / TOKENS
        whole = lax.all_gather(moment, ("core", "y", "zl"), axis=0, tiled=True)

    with jax.named_scope("gram"):
        local_gram = lax.dot_general(
            moment, moment, over_tokens, precision=lax.Precision.HIGHEST
        )
        strip = jnp.sum(swap(local_gram.reshape(32, K // 32, K), ("zl", "core", "x")), axis=0)
        strip = jnp.sum(share(strip, "y"), axis=0)
        gram = share(strip, ("zl", "core", "x")).reshape(K, K)

    with jax.named_scope("new_basis"):
        inverse = inverse_factor(gram)
        solved = lax.dot_general(
            whole, inverse, (((1,), (1,)), ((), ())), precision=lax.Precision.HIGH
        )
        return (solved * math.sqrt(D)).astype(jnp.bfloat16)


def solution(mesh):
    fine = Mesh(mesh.devices.reshape(3, 4, 8, 2, 4), TOK + ("x",))
    return jax.shard_map(
        on_device,
        mesh=fine,
        in_specs=(P(TOK, "x"), P("x", None)),
        out_specs=P("x", None),
        check_vma=False,
    )
```

```python
import math

import jax
import jax.numpy as jnp
from jax import lax
from jax.experimental import pallas as pl
from jax.experimental.pallas import tpu as pltpu
from jax.sharding import Mesh, PartitionSpec as P

D = 8192
K = 256
TOKENS = 49152
BLOCK = 8
TOK = ("zh", "zl", "y", "core")


def inverse_factor_kernel(gram_ref, out_ref, work):
    work[...] = gram_ref[...]
    lane = lax.broadcasted_iota(jnp.int32, (BLOCK, K), 1)
    row_of = lax.broadcasted_iota(jnp.int32, (BLOCK, K), 0)

    def wide(value):
        return jnp.concatenate([value, value], axis=1)

    def column(block, k):
        return jnp.broadcast_to(block[:, k : k + 1], (BLOCK, 128))

    for j in range(0, K, BLOCK):
        inside = (lane >= j) & (lane < j + BLOCK)
        rows = work[j : j + BLOCK, :]
        columns = [column(rows, j + c) for c in range(BLOCK)]
        left = {
            (r, c): jnp.broadcast_to(columns[c][r : r + 1, :], (BLOCK, 128))
            for c in range(BLOCK)
            for r in range(c, BLOCK)
        }
        near = j + BLOCK if j + BLOCK < K else None
        if near is not None:
            below = work[near : near + BLOCK, :]
            below_columns = [column(below, j + c) for c in range(BLOCK)]
            new = jnp.where(inside, 0.0, below)
        scale, low, solved = [], {}, []
        for t in range(BLOCK):
            inv = lax.rsqrt(left[t, t])
            narrow = {r: left[r, t] * inv for r in range(t + 1, BLOCK)}
            for c in range(t + 1, BLOCK):
                for r in range(c, BLOCK):
                    left[r, c] = left[r, c] - narrow[r] * narrow[c]
            for r, value in narrow.items():
                low[r, t] = wide(value)
            scale.append(wide(inv))
            row = jnp.broadcast_to(rows[t : t + 1, :], (BLOCK, K))
            row = jnp.where(inside, jnp.where(lane == j + t, 1.0, 0.0), row)
            for s in range(t):
                row = row - low[t, s] * solved[s]
            solved.append(row * scale[t])
            if near is not None:
                factor = below_columns[t] * inv
                for c in range(t + 1, BLOCK):
                    below_columns[c] = below_columns[c] - factor * narrow[c]
                new = new - wide(factor) * solved[t]
        if near is not None:
            work[near : near + BLOCK, :] = new
        if j + 2 * BLOCK < K:
            update = [None] * BLOCK
            for t in reversed(range(BLOCK)):
                row = solved[t]
                for s in range(t + 1, BLOCK):
                    row = row - low[s, t] * update[s]
                update[t] = row * scale[t]
            for i in range(j + 2 * BLOCK, K, BLOCK):
                below = work[i : i + BLOCK, :]
                new = jnp.where(inside, 0.0, below)
                for t in range(BLOCK):
                    new = new - jnp.broadcast_to(below[:, j + t : j + t + 1], (BLOCK, K)) * update[t]
                work[i : i + BLOCK, :] = new
        result = solved[0]
        for t in range(1, BLOCK):
            result = jnp.where(row_of == t, solved[t], result)
        out_ref[j : j + BLOCK, :] = jnp.where(lane < j + BLOCK, result, 0.0)


def inverse_factor(gram):
    return pl.pallas_call(
        inverse_factor_kernel,
        out_shape=jax.ShapeDtypeStruct((K, K), jnp.float32),
        in_specs=[pl.BlockSpec(memory_space=pltpu.VMEM)],
        out_specs=pl.BlockSpec(memory_space=pltpu.VMEM),
        scratch_shapes=[pltpu.VMEM((K, K), jnp.float32)],
        cost_estimate=pl.CostEstimate(flops=40_000_000, bytes_accessed=524_288, transcendentals=K),
    )(gram)


def swap(pieces, axis):
    return lax.all_to_all(pieces, axis, 0, 0, tiled=True)


def share(block, axis):
    return swap(jnp.broadcast_to(block[None], (lax.axis_size(axis),) + block.shape), axis)


def on_device(activations, sketch):
    tok_rows, panel = activations.shape
    half = panel // 2
    core = lax.axis_index("core")
    kept = lax.dynamic_slice_in_dim(activations, core * half, half, axis=1)
    given = lax.dynamic_slice_in_dim(activations, (1 - core) * half, half, axis=1)
    other = lax.ppermute(given, "core", [(0, 1), (1, 0)])

    with jax.named_scope("projected"):
        partial_sum = jnp.dot(activations, sketch, preferred_element_type=jnp.float32)
        summed = jnp.sum(swap(partial_sum.reshape(4, tok_rows // 4, K), "x"), axis=0)
        rows = (summed * (1.0 / math.sqrt(D))).astype(jnp.bfloat16)
        projected = share(rows, ("core", "x")).reshape(2, tok_rows, K)
        own = lax.dynamic_index_in_dim(projected, core, axis=0, keepdims=False)
        others = lax.dynamic_index_in_dim(projected, 1 - core, axis=0, keepdims=False)

    with jax.named_scope("moment"):
        over_tokens = (((0,), (0,)), ((), ()))
        chip_sum = lax.dot_general(
            kept, own, over_tokens, preferred_element_type=jnp.float32
        ) + lax.dot_general(other, others, over_tokens, preferred_element_type=jnp.float32)
        pieces = chip_sum.astype(jnp.bfloat16).reshape(32, half // 32, K)
        part = jnp.sum(swap(pieces, ("y", "zl")).astype(jnp.float32), axis=0)
        part = jnp.sum(share(part, "zh"), axis=0)
        moment = share(part, "zl").reshape(half // 8, K) / TOKENS
        whole = lax.all_gather(moment, ("core", "y"), axis=0, tiled=True)

    with jax.named_scope("gram"):
        local_gram = lax.dot_general(
            moment, moment, over_tokens, precision=lax.Precision.HIGHEST
        )
        quarter = lax.dynamic_slice_in_dim(
            local_gram, lax.axis_index("zl") * (K // 4), K // 4, axis=0
        )
        strip = jnp.sum(swap(quarter.reshape(8, K // 32, K), ("core", "x")), axis=0)
        strip = jnp.sum(share(strip, "y"), axis=0)
        gram = share(strip, ("zl", "core", "x")).reshape(K, K)

    with jax.named_scope("new_basis"):
        inverse = inverse_factor(gram)
        solved = lax.dot_general(
            whole, inverse, (((1,), (1,)), ((), ())), precision=lax.Precision.HIGH
        )
        return (solved * math.sqrt(D)).astype(jnp.bfloat16)


def solution(mesh):
    fine = Mesh(mesh.devices.reshape(3, 4, 8, 2, 4), TOK + ("x",))
    return jax.shard_map(
        on_device,
        mesh=fine,
        in_specs=(P(TOK, "x"), P("x", None)),
        out_specs=P("x", None),
        check_vma=False,
    )
```

```python
import math

import jax
import jax.numpy as jnp
from jax import lax
from jax.experimental import pallas as pl
from jax.experimental.pallas import tpu as pltpu
from jax.sharding import Mesh, PartitionSpec as P

D = 8192
K = 256
TOKENS = 49152
BLOCK = 8
TOK = ("zh", "zm", "zl", "y", "core")


def inverse_factor_kernel(gram_ref, out_ref, work):
    work[...] = gram_ref[...]
    lane = lax.broadcasted_iota(jnp.int32, (BLOCK, K), 1)
    row_of = lax.broadcasted_iota(jnp.int32, (BLOCK, K), 0)

    def wide(value):
        return jnp.concatenate([value, value], axis=1)

    def column(block, k):
        return jnp.broadcast_to(block[:, k : k + 1], (BLOCK, 128))

    for j in range(0, K, BLOCK):
        inside = (lane >= j) & (lane < j + BLOCK)
        rows = work[j : j + BLOCK, :]
        columns = [column(rows, j + c) for c in range(BLOCK)]
        left = {
            (r, c): jnp.broadcast_to(columns[c][r : r + 1, :], (BLOCK, 128))
            for c in range(BLOCK)
            for r in range(c, BLOCK)
        }
        near = j + BLOCK if j + BLOCK < K else None
        if near is not None:
            below = work[near : near + BLOCK, :]
            below_columns = [column(below, j + c) for c in range(BLOCK)]
            new = jnp.where(inside, 0.0, below)
        scale, low, solved = [], {}, []
        for t in range(BLOCK):
            inv = lax.rsqrt(left[t, t])
            narrow = {r: left[r, t] * inv for r in range(t + 1, BLOCK)}
            for c in range(t + 1, BLOCK):
                for r in range(c, BLOCK):
                    left[r, c] = left[r, c] - narrow[r] * narrow[c]
            for r, value in narrow.items():
                low[r, t] = wide(value)
            scale.append(wide(inv))
            row = jnp.broadcast_to(rows[t : t + 1, :], (BLOCK, K))
            row = jnp.where(inside, jnp.where(lane == j + t, 1.0, 0.0), row)
            for s in range(t):
                row = row - low[t, s] * solved[s]
            solved.append(row * scale[t])
            if near is not None:
                factor = below_columns[t] * inv
                for c in range(t + 1, BLOCK):
                    below_columns[c] = below_columns[c] - factor * narrow[c]
                new = new - wide(factor) * solved[t]
        if near is not None:
            work[near : near + BLOCK, :] = new
        if j + 2 * BLOCK < K:
            update = [None] * BLOCK
            for t in reversed(range(BLOCK)):
                row = solved[t]
                for s in range(t + 1, BLOCK):
                    row = row - low[s, t] * update[s]
                update[t] = row * scale[t]
            for i in range(j + 2 * BLOCK, K, BLOCK):
                below = work[i : i + BLOCK, :]
                new = jnp.where(inside, 0.0, below)
                for t in range(BLOCK):
                    new = new - jnp.broadcast_to(below[:, j + t : j + t + 1], (BLOCK, K)) * update[t]
                work[i : i + BLOCK, :] = new
        result = solved[0]
        for t in range(1, BLOCK):
            result = jnp.where(row_of == t, solved[t], result)
        out_ref[j : j + BLOCK, :] = jnp.where(lane < j + BLOCK, result, 0.0)


def inverse_factor(gram):
    return pl.pallas_call(
        inverse_factor_kernel,
        out_shape=jax.ShapeDtypeStruct((K, K), jnp.float32),
        in_specs=[pl.BlockSpec(memory_space=pltpu.VMEM)],
        out_specs=pl.BlockSpec(memory_space=pltpu.VMEM),
        scratch_shapes=[pltpu.VMEM((K, K), jnp.float32)],
        cost_estimate=pl.CostEstimate(flops=40_000_000, bytes_accessed=524_288, transcendentals=K),
    )(gram)


def swap(pieces, axis):
    return lax.all_to_all(pieces, axis, 0, 0, tiled=True)


def share(block, axis):
    return swap(jnp.broadcast_to(block[None], (lax.axis_size(axis),) + block.shape), axis)


def on_device(activations, sketch):
    tok_rows, panel = activations.shape
    half = panel // 2
    core = lax.axis_index("core")
    kept = lax.dynamic_slice_in_dim(activations, core * half, half, axis=1)
    given = lax.dynamic_slice_in_dim(activations, (1 - core) * half, half, axis=1)
    other = lax.ppermute(given, "core", [(0, 1), (1, 0)])

    with jax.named_scope("projected"):
        partial_sum = jnp.dot(activations, sketch, preferred_element_type=jnp.float32)
        terms = share(partial_sum.astype(jnp.bfloat16), "x").astype(jnp.float32)
        own = (jnp.sum(terms, axis=0) * (1.0 / math.sqrt(D))).astype(jnp.bfloat16)
        others = lax.ppermute(own, "core", [(0, 1), (1, 0)])

    with jax.named_scope("moment"):
        over_tokens = (((0,), (0,)), ((), ()))
        chip_sum = lax.dot_general(
            kept, own, over_tokens, preferred_element_type=jnp.float32
        ) + lax.dot_general(other, others, over_tokens, preferred_element_type=jnp.float32)
        pieces = chip_sum.astype(jnp.bfloat16).reshape(32, half // 32, K)
        part = jnp.sum(swap(pieces, ("y", "zm", "zl")).astype(jnp.float32), axis=0)
        part = jnp.sum(share(part, "zh"), axis=0)
        moment = share(part, ("zm", "zl")).reshape(half // 8, K) / TOKENS
        whole = lax.all_gather(moment, ("core", "y"), axis=0, tiled=True)

    with jax.named_scope("gram"):
        local_gram = lax.dot_general(
            moment, moment, over_tokens, precision=lax.Precision.HIGHEST
        )
        part_gram = lax.dynamic_slice_in_dim(
            local_gram, lax.axis_index("zl") * (K // 2), K // 2, axis=0
        )
        strip = jnp.sum(swap(part_gram.reshape(8, K // 16, K), ("core", "x")), axis=0)
        strip = jnp.sum(share(strip, "y"), axis=0)
        gram = share(strip, ("zl", "core", "x")).reshape(K, K)

    with jax.named_scope("new_basis"):
        inverse = inverse_factor(gram)
        solved = lax.dot_general(
            whole, inverse, (((1,), (1,)), ((), ())), precision=lax.Precision.HIGH
        )
        return (solved * math.sqrt(D)).astype(jnp.bfloat16)


def solution(mesh):
    fine = Mesh(mesh.devices.reshape(3, 2, 2, 8, 2, 4), TOK + ("x",))
    return jax.shard_map(
        on_device,
        mesh=fine,
        in_specs=(P(TOK, "x"), P("x", None)),
        out_specs=P("x", None),
        check_vma=False,
    )
```

```python
import math

import jax
import jax.numpy as jnp
from jax import lax
from jax.experimental import pallas as pl
from jax.experimental.pallas import tpu as pltpu
from jax.sharding import Mesh, PartitionSpec as P

D = 8192
K = 256
TOKENS = 49152
BLOCK = 8
TOK = ("zh", "zm", "zl", "y", "core")


def inverse_factor_kernel(gram_ref, out_ref, work):
    work[...] = gram_ref[...]
    lane = lax.broadcasted_iota(jnp.int32, (BLOCK, K), 1)
    row_of = lax.broadcasted_iota(jnp.int32, (BLOCK, K), 0)

    def wide(value):
        return jnp.concatenate([value, value], axis=1)

    def column(block, k):
        return jnp.broadcast_to(block[:, k : k + 1], (BLOCK, 128))

    for j in range(0, K, BLOCK):
        inside = (lane >= j) & (lane < j + BLOCK)
        rows = work[j : j + BLOCK, :]
        columns = [column(rows, j + c) for c in range(BLOCK)]
        left = {
            (r, c): jnp.broadcast_to(columns[c][r : r + 1, :], (BLOCK, 128))
            for c in range(BLOCK)
            for r in range(c, BLOCK)
        }
        near = j + BLOCK if j + BLOCK < K else None
        if near is not None:
            below = work[near : near + BLOCK, :]
            below_columns = [column(below, j + c) for c in range(BLOCK)]
            new = jnp.where(inside, 0.0, below)
        scale, low, solved = [], {}, []
        for t in range(BLOCK):
            inv = lax.rsqrt(left[t, t])
            narrow = {r: left[r, t] * inv for r in range(t + 1, BLOCK)}
            for c in range(t + 1, BLOCK):
                for r in range(c, BLOCK):
                    left[r, c] = left[r, c] - narrow[r] * narrow[c]
            for r, value in narrow.items():
                low[r, t] = wide(value)
            scale.append(wide(inv))
            row = jnp.broadcast_to(rows[t : t + 1, :], (BLOCK, K))
            row = jnp.where(inside, jnp.where(lane == j + t, 1.0, 0.0), row)
            for s in range(t):
                row = row - low[t, s] * solved[s]
            solved.append(row * scale[t])
            if near is not None:
                factor = below_columns[t] * inv
                for c in range(t + 1, BLOCK):
                    below_columns[c] = below_columns[c] - factor * narrow[c]
                new = new - wide(factor) * solved[t]
        if near is not None:
            work[near : near + BLOCK, :] = new
        if j + 2 * BLOCK < K:
            update = [None] * BLOCK
            for t in reversed(range(BLOCK)):
                row = solved[t]
                for s in range(t + 1, BLOCK):
                    row = row - low[s, t] * update[s]
                update[t] = row * scale[t]
            for i in range(j + 2 * BLOCK, K, BLOCK):
                below = work[i : i + BLOCK, :]
                new = jnp.where(inside, 0.0, below)
                for t in range(BLOCK):
                    new = new - jnp.broadcast_to(below[:, j + t : j + t + 1], (BLOCK, K)) * update[t]
                work[i : i + BLOCK, :] = new
        result = solved[0]
        for t in range(1, BLOCK):
            result = jnp.where(row_of == t, solved[t], result)
        out_ref[j : j + BLOCK, :] = jnp.where(lane < j + BLOCK, result, 0.0)


def inverse_factor(gram):
    return pl.pallas_call(
        inverse_factor_kernel,
        out_shape=jax.ShapeDtypeStruct((K, K), jnp.float32),
        in_specs=[pl.BlockSpec(memory_space=pltpu.VMEM)],
        out_specs=pl.BlockSpec(memory_space=pltpu.VMEM),
        scratch_shapes=[pltpu.VMEM((K, K), jnp.float32)],
        cost_estimate=pl.CostEstimate(flops=40_000_000, bytes_accessed=524_288, transcendentals=K),
    )(gram)


def swap(pieces, axis):
    return lax.all_to_all(pieces, axis, 0, 0, tiled=True)


def share(block, axis):
    return swap(jnp.broadcast_to(block[None], (lax.axis_size(axis),) + block.shape), axis)


def on_device(activations, sketch):
    tok_rows, panel = activations.shape
    half = panel // 2
    core = lax.axis_index("core")
    kept = lax.dynamic_slice_in_dim(activations, core * half, half, axis=1)
    given = lax.dynamic_slice_in_dim(activations, (1 - core) * half, half, axis=1)
    other = lax.ppermute(given, "core", [(0, 1), (1, 0)])

    with jax.named_scope("projected"):
        partial_sum = jnp.dot(activations, sketch, preferred_element_type=jnp.float32)
        terms = share(partial_sum.astype(jnp.bfloat16), "x").astype(jnp.float32)
        own = (jnp.sum(terms, axis=0) * (1.0 / math.sqrt(D))).astype(jnp.bfloat16)
        others = lax.ppermute(own, "core", [(0, 1), (1, 0)])

    with jax.named_scope("moment"):
        over_tokens = (((0,), (0,)), ((), ()))
        chip_sum = lax.dot_general(
            kept, own, over_tokens, preferred_element_type=jnp.float32
        ) + lax.dot_general(other, others, over_tokens, preferred_element_type=jnp.float32)
        pieces = chip_sum.astype(jnp.bfloat16).reshape(32, half // 32, K)
        part = jnp.sum(swap(pieces, ("y", "zm", "zl")).astype(jnp.float32), axis=0)
        part = jnp.sum(share(part, "zh"), axis=0) / TOKENS
        moment = share(part, ("zm", "zl")).reshape(half // 8, K)
        whole = lax.all_gather(moment, ("core", "y"), axis=0, tiled=True)

    with jax.named_scope("gram"):
        local_gram = lax.dot_general(
            moment, moment, over_tokens, precision=lax.Precision.HIGHEST
        )
        part_gram = lax.dynamic_slice_in_dim(
            local_gram, lax.axis_index("zl") * (K // 2), K // 2, axis=0
        )
        strip = jnp.sum(swap(part_gram.reshape(8, K // 16, K), ("core", "x")), axis=0)
        strip = jnp.sum(share(strip, "y"), axis=0)
        gram = share(strip, ("zl", "core", "x")).reshape(K, K)

    with jax.named_scope("new_basis"):
        inverse = inverse_factor(gram)
        solved = lax.dot_general(
            whole, inverse, (((1,), (1,)), ((), ())), precision=lax.Precision.HIGH
        )
        return (solved * math.sqrt(D)).astype(jnp.bfloat16)


def solution(mesh):
    fine = Mesh(mesh.devices.reshape(3, 2, 2, 8, 2, 4), TOK + ("x",))
    return jax.shard_map(
        on_device,
        mesh=fine,
        in_specs=(P(TOK, "x"), P("x", None)),
        out_specs=P("x", None),
        check_vma=False,
    )
```
